32 devices in a mesh: groups: 2 (over y), rows: 8 (over z, core), cols: 2 (over x).
Axes of the slice: x: 2, y: 2, z: 4, core: 2. Of those that a mesh axis runs over, the one named last changes fastest.
Arguments:
- big_emb: bfloat16 [8192, 768], P(('groups', 'rows', 'cols')), parts along dimension 0, may hold values from -6 to 6
- big_order: int32 [8192], P(('groups', 'rows', 'cols')), parts along dimension 0, may hold values from 0 to 4095, each once
- small_emb: bfloat16 [32, 8, 16, 768], P(('groups', 'rows', 'cols')), parts along dimension 0, may hold values from -6 to 6
- small_clus: int32 [32, 8, 16], P(('groups', 'rows', 'cols')), parts along dimension 0, may hold values from -1 to 15, as said below
- small_order: int32 [32, 8, 16], P(('groups', 'rows', 'cols')), parts along dimension 0, may hold values from 0 to 2047, as said below
Outputs:
- big_best: float32 [8192], P(('groups', 'rows', 'cols')), parts along dimension 0
- small_best: float32 [32, 8, 16], P(('groups', 'rows', 'cols')), parts along dimension 0
The draws below stay inside these ranges and needn't reach their ends.
There are 2 independent parts, one for each index of `groups`. The reference program is written for one: setup_inputs(seed, part) draws one part's arguments, and reference() takes and returns one part's arrays. A program takes and returns all parts, laid end to end along the dimension named above; each array names one. Nothing has to cross between parts.
Inputs may be any that keep to these rules, and one draw needn't show every extreme that they name: `small_clus`: -1 marks an empty slot; otherwise one of the 16 clusters of the destination device. The slots to one destination from one source are at most 16 live, and in every draw some source fills all 16 slots to some destination. `small_order`: each value occurs once within each part within each part (each index of `groups`).
All inputs are finite; a program needn't handle non-finite values.
Results may differ from the reference program's by a relative error of at most 0.0012.
Values may be sent and summed in bfloat16 or wider, within the bound.
A program may use at most 64 MiB of HBM per device.

```python
import jax
import jax.numpy as jnp
from jax import lax

D = 768
CAP = 16
KCL = 16
BIG = 4096
SRC = 16
N_ROWS = 8
N_COLS = 2


def draw_small_clus(key, part):
    base = jax.random.fold_in(key, 11)
    key_live, key_full, key_ids = jax.random.split(base, 3)
    pairs = N_ROWS * N_COLS * N_ROWS
    live = jax.random.randint(key_live, (pairs,), CAP // 3, CAP, dtype=jnp.int32)
    full_pair = jax.random.randint(key_full, (), 0, pairs, dtype=jnp.int32)
    live = jnp.where(jnp.arange(pairs, dtype=jnp.int32) == full_pair, CAP, live)
    ids = jax.random.randint(key_ids, (pairs, CAP), 0, KCL, dtype=jnp.int32)
    ids = ids.at[full_pair, 0].set(KCL - 1)
    slot_index = jnp.arange(CAP, dtype=jnp.int32)
    result = jnp.where(slot_index[None, :] < live[:, None], ids, -1)
    return result.reshape(N_ROWS * N_COLS, N_ROWS, CAP).astype(jnp.int32)


def draw_small_order(key, part):
    base = jax.random.fold_in(key, 23)
    total = N_ROWS * N_COLS * N_ROWS * CAP
    ranks = jax.random.permutation(base, jnp.arange(total, dtype=jnp.int32))
    return ranks.reshape(N_ROWS * N_COLS, N_ROWS, CAP).astype(jnp.int32)


def levels(rng, dims, cuts, smallest, high):
    factor_of = 1.0
    for axis_at, shards_of in cuts:
        draws = jax.random.uniform(jax.random.fold_in(jax.random.fold_in(rng, 6), axis_at), (shards_of,), jnp.float32, smallest / len(cuts), high / len(cuts))
        factor_of = factor_of * jnp.repeat(jnp.exp(draws), dims[axis_at] // shards_of).reshape((-1,) + (1,) * (len(dims) - 1 - axis_at))
    return factor_of


def centred(rng, shape, scale, bound, cuts=(), kind=jnp.bfloat16):
    array = jax.random.normal(rng, shape, jnp.float32) * scale
    if len(cuts) > 0:
        array = levels(rng, shape, cuts, -0.22, 0.18) * array
    return jnp.clip(array, min=-bound, max=bound).astype(kind)


def setup_inputs(seed: int = 0, part: int = 0) -> dict:
    streams_of = jax.random.split(jax.random.key(seed), 6)
    part_keys = jax.random.split(jax.random.fold_in(streams_of[5], part), 6)
    big_emb = centred(part_keys[0], (BIG, D), 1.0, 6.0, ((0, 16),))
    big_order = jax.random.permutation(part_keys[1], BIG).astype(jnp.int32)
    small_emb = centred(part_keys[2], (SRC, N_ROWS, CAP, D), 1.0, 6.0, ((0, 16),))
    small_clus = draw_small_clus(jax.random.fold_in(jax.random.fold_in(streams_of[5], part), 71), part)
    small_order = draw_small_order(jax.random.fold_in(jax.random.fold_in(streams_of[5], part), 71), part)
    return dict(big_emb=big_emb, big_order=big_order, small_emb=small_emb, small_clus=small_clus, small_order=small_order)


def normalize(values):
    floats = values.astype(jnp.float32)
    squares = lax.optimization_barrier(jnp.sum(floats * floats, axis=-1, keepdims=True))
    return (floats * lax.rsqrt(squares + 1e-06)).astype(jnp.bfloat16)

def best_over(row_emb, row_ord, col_emb, col_ord):
    total_rows = row_emb.shape[0]
    height = 512 if total_rows % 512 == 0 else total_rows

    def one_block(block_at):
        rows_here = lax.dynamic_slice_in_dim(row_emb, block_at * height, height, 0)
        ord_here = lax.dynamic_slice_in_dim(row_ord, block_at * height, height, 0)
        scores = lax.dot_general(rows_here, col_emb, (((1,), (1,)), ((), ())), preferred_element_type=jnp.float32)
        allowed = col_ord[None, :] < ord_here[:, None]
        return lax.optimization_barrier(jnp.max(jnp.where(allowed, scores, jnp.float32(-1.0)), axis=1))
    blocks = lax.map(one_block, jnp.arange(total_rows // height, dtype=jnp.int32))
    return jnp.maximum(blocks.reshape(total_rows), jnp.float32(-1.0))

def cluster_best(slots, clusters, orders):
    scores = lax.dot_general(slots, slots, (((1,), (1,)), ((), ())), preferred_element_type=jnp.float32)
    allowed = (clusters[None, :] == clusters[:, None]) & (clusters[:, None] >= 0) & (orders[None, :] < orders[:, None])
    return lax.optimization_barrier(jnp.max(jnp.where(allowed, scores, jnp.float32(-1.0)), axis=1))

def reference(big_emb, big_order, small_emb, small_clus, small_order):
    big_unit = normalize(big_emb)
    big_best = best_over(big_unit, big_order, big_unit, big_order)
    small_unit = normalize(small_emb)
    emb_five = small_unit.reshape(N_ROWS, N_COLS, N_ROWS, CAP, D).transpose(2, 1, 0, 3, 4)
    emb_dest = emb_five.reshape(N_ROWS * N_COLS, N_ROWS * CAP, D)
    clus_dest = small_clus.reshape(N_ROWS, N_COLS, N_ROWS, CAP).transpose(2, 1, 0, 3).reshape(N_ROWS * N_COLS, N_ROWS * CAP)
    ord_dest = small_order.reshape(N_ROWS, N_COLS, N_ROWS, CAP).transpose(2, 1, 0, 3).reshape(N_ROWS * N_COLS, N_ROWS * CAP)

    def per_dest(inputs):
        return cluster_best(inputs[0], inputs[1], inputs[2])
    results = lax.map(per_dest, (emb_dest, clus_dest, ord_dest))
    small_best = results.reshape(N_ROWS, N_COLS, N_ROWS, CAP).transpose(2, 1, 0, 3).reshape(N_ROWS * N_COLS, N_ROWS, CAP)
    return (big_best, small_best)
```

```python
import functools

import jax
import jax.numpy as jnp
from jax import lax
from jax.experimental import pallas as pl
from jax.experimental.pallas import tpu as pltpu
from jax.sharding import PartitionSpec as P

LANES = 128
MESH = pl.DeviceIdType.MESH


def normalize(values):
    floats = values.astype(jnp.float32)
    squares = jnp.sum(floats * floats, axis=-1, keepdims=True)
    return (floats * lax.rsqrt(squares + 1e-06)).astype(jnp.bfloat16)


def upright(row):
    return jnp.broadcast_to(row, (LANES, LANES)).T


def kernel(
    n_rows, n_cols,
    be, bo, se, sc, so, out_b, out_s,
    col_buf, row_buf, row_ord, meta_s, meta_r, sm_s, sm_r, acc, pm_s, pm_r, cm_s, cm_r, rs_s, rs_r, pad,
    recv, up_sem, down_sem, core_sem, x_send, x_recv, xo_send, xo_recv,
    me_send, me_recv, sm_send, sm_recv, rs_send, rs_recv, pm_send, pm_recv, cm_send, cm_recv,
):
    r = lax.axis_index("rows")
    c = lax.axis_index("cols")
    z, core = r // 2, r % 2
    partner = z * 2 + 1 - core
    depth, half = n_rows // 2, n_rows // 4
    block = be.shape[0]
    chunks = block // LANES
    cap = se.shape[2]
    width = rs_s.shape[1]

    def peers(count, me, body):
        def one(d, carry):
            body(lax.rem(me + d, count))
            return carry
        lax.fori_loop(1, count, one, 0)

    barrier = pltpu.get_barrier_semaphore()
    peers(n_rows, r, lambda p: pl.semaphore_signal(barrier, inc=1, device_id={"rows": p}, device_id_type=MESH))
    peers(n_cols, c, lambda p: pl.semaphore_signal(barrier, inc=1, device_id={"cols": p}, device_id_type=MESH))

    def remote(src, dst, send, recv_sem, axis, to):
        return pltpu.make_async_remote_copy(
            src_ref=src, dst_ref=dst, send_sem=send, recv_sem=recv_sem, device_id={axis: to}, device_id_type=MESH
        )

    def part(b, k):
        return col_buf.at[b, pl.ds(k * LANES, LANES), :]

    def hop(b, k, sems, to):
        return remote(part(b, k), part(b, k), sems.at[b // 2, k], recv.at[b, k], "rows", to)

    def x_copy(k, to, owner):
        lines = pl.ds(k * LANES, LANES)
        return remote(part(r, k), row_buf.at[owner, lines, :], x_send.at[to, k], x_recv.at[owner, k], "cols", to)

    def xo_copy(to, owner):
        return remote(bo, row_ord.at[owner], xo_send.at[to], xo_recv.at[owner], "cols", to)

    def me_copy(to, owner):
        return remote(meta_s.at[to], meta_r.at[owner], me_send.at[to], me_recv.at[owner], "rows", to)

    def sm_copy(to, owner):
        return remote(sm_s.at[to], sm_r.at[owner], sm_send.at[to], sm_recv.at[owner], "rows", to)

    def rs_copy(to, owner):
        return remote(rs_s, rs_r.at[owner], rs_send.at[to], rs_recv.at[owner], "rows", to)

    def pm_copy(to, owner):
        return remote(pm_s.at[to], pm_r.at[owner], pm_send.at[to], pm_recv.at[owner], "cols", to)

    def cm_copy(to, owner):
        return remote(cm_s.at[to], cm_r.at[owner], cm_send.at[to], cm_recv.at[owner], "rows", to)

    def below_ok(s):
        return (z - s >= 0) & (z - s < half)

    def above_ok(s):
        return (z + s < depth) & (z >= half)

    for k in range(chunks):
        lines = pl.ds(k * LANES, LANES)
        unit = normalize(be[lines, :])
        col_buf[r, lines, :] = unit
        row_buf[c, lines, :] = unit
        if k == 0:
            pl.semaphore_wait(barrier, n_rows - 1 + n_cols - 1)

        @pl.when(z < half)
        def _():
            hop(r, k, up_sem, r + 2).start()

        @pl.when(z > half)
        def _():
            hop(r, k, down_sem, r - 2).start()

        hop(r, k, core_sem, partner).start()
        peers(n_cols, c, lambda p: x_copy(k, p, c).start())

    row_ord[c] = bo[...]
    peers(n_cols, c, lambda p: xo_copy(p, c).start())

    pad[...] = jnp.zeros_like(pad)
    pad[0, :, :cap] = sc[0]
    pad[1, :, :cap] = so[0]
    clus = pltpu.roll(pad[0], r * cap, 1)
    order = pltpu.roll(pad[1], r * cap, 1)
    for p in range(n_rows):
        meta_s[p, 0:1, :block] = bo[...]
        meta_s[p, 1:2, :width] = clus[p:p + 1, :]
        meta_s[p, 2:3, :width] = order[p:p + 1, :]
    peers(n_rows, r, lambda p: me_copy(p, r).start())
    sm_s[...] = normalize(se[0])
    peers(n_rows, r, lambda p: sm_copy(p, r).start())
    meta_r[r] = meta_s[r]
    sm_r[r] = sm_s[r]
    acc[...] = jnp.full(acc.shape, -1.0, jnp.float32)

    def forward(s, k):
        @pl.when(below_ok(s))
        def _():
            b = r - 2 * s
            hop(b, k, core_sem, partner).wait_recv()

            @pl.when(z < depth - 1)
            def _():
                hop(b, k, up_sem, r + 2).start()

            hop(b, k, core_sem, partner).start()

        @pl.when(above_ok(s))
        def _():
            b = r + 2 * s
            hop(b, k, core_sem, partner).wait_recv()

            @pl.when(z > half)
            def _():
                hop(b, k, down_sem, r - 2).start()

            hop(b, k, core_sem, partner).start()

    def scores_of(b, k, both):
        at = pl.ds(k * LANES, LANES)
        ord_col = upright(meta_r[b, 0:1, at])
        rows = row_buf[...].reshape(n_cols * block, row_buf.shape[2])
        scores = lax.dot_general(
            col_buf[b, at, :], rows, (((1,), (1,)), ((), ())), preferred_element_type=jnp.float32
        )
        best = jnp.full((LANES, LANES), -1.0, jnp.float32)
        for tile in range(n_cols * block // LANES):
            lanes = slice(tile * LANES, (tile + 1) * LANES)
            here = scores[:, lanes]
            lane = (tile * LANES) % block
            ord_row = row_ord[tile * LANES // block, 0:1, lane:lane + LANES]
            kept = jnp.where(ord_col < ord_row, here, jnp.float32(-1.0))
            acc[:, lanes] = jnp.maximum(acc[:, lanes], jnp.max(kept.reshape(LANES // 8, 8, LANES), axis=0))
            if both:
                best = jnp.maximum(best, jnp.where(ord_row < ord_col, here, jnp.float32(-1.0)))
        if both:
            cm_s[b, 0:1, at] = jnp.max(best.T, axis=0, keepdims=True)

    def pair(b, k):
        other = (b // 2) * 2 + 1 - core
        hop(other, k, core_sem, partner).wait_recv()
        scores_of(b, k, True)
        scores_of(other, k, True)
        if k == chunks - 1:
            cm_copy(b, r).start()
            cm_copy(other, r).start()

    def pairs(s, k):
        @pl.when(below_ok(s))
        def _():
            pair(r - 2 * s, k)

        @pl.when(above_ok(s))
        def _():
            pair(r + 2 * s, k)

    if depth > 1:
        for k in range(chunks):
            forward(1, k)
    for k in range(chunks):
        peers(n_cols, c, lambda p: x_copy(k, p, p).wait_recv())
    peers(n_cols, c, lambda p: xo_copy(p, p).wait_recv())
    peers(n_rows, r, lambda p: me_copy(p, p).wait_recv())
    for k in range(chunks):
        scores_of(r, k, False)
        hop(partner, k, core_sem, partner).wait_recv()
        scores_of(partner, k, False)

    peers(n_rows, r, lambda p: sm_copy(p, p).wait_recv())
    slots = n_rows * cap
    clus_row = jnp.sum(meta_r[:, 1, :width], axis=0, keepdims=True)
    ord_row = jnp.sum(meta_r[:, 2, :width], axis=0, keepdims=True)
    emb = sm_r[...].reshape(slots, sm_r.shape[2])
    best = jnp.full((1, width), -1.0, jnp.float32)
    for at in range(0, slots, LANES):
        scores = lax.dot_general(
            emb[at:at + LANES], emb, (((1,), (1,)), ((), ())), preferred_element_type=jnp.float32
        )
        clus_col = jnp.broadcast_to(upright(clus_row[:, at:at + LANES])[:, :1], (LANES, width))
        ord_col = jnp.broadcast_to(upright(ord_row[:, at:at + LANES])[:, :1], (LANES, width))
        allowed = (clus_col == clus_row) & (clus_row >= 0) & (ord_col < ord_row)
        kept = jnp.where(allowed, scores, jnp.float32(-1.0))
        best = jnp.maximum(best, jnp.max(kept, axis=0, keepdims=True))
    rs_s[...] = best
    rs_r[r] = best
    peers(n_rows, r, lambda p: rs_copy(p, r).start())

    def step(s, carry):
        for k in range(chunks):
            forward(s, k)
            pairs(s - 1, k)
        return carry

    lax.fori_loop(2, depth, step, 0)
    for k in range(chunks):
        pairs(depth - 1, k)

    final = jnp.max(acc[...], axis=0, keepdims=True)
    for p in range(n_cols):
        pm_s[p] = final[:, p * block:(p + 1) * block]
    peers(n_cols, c, lambda p: pm_copy(p, c).start())

    peers(n_rows, r, lambda p: rs_copy(p, p).wait_recv())
    back = pltpu.roll(rs_r[:, 0, :], lax.rem(width - r * cap, width), 1)
    out_s[0] = back[:, :cap]

    out_b[...] = pm_s[c]

    def returned(p, carry):
        zp = p // 2
        low = (z < half) & (zp > z)
        high = (z >= half) & (zp >= half) & (zp < z)

        @pl.when(low | high)
        def _():
            cm_copy(p, p).wait_recv()
            out_b[...] = jnp.maximum(out_b[...], cm_r[p])
        return carry

    lax.fori_loop(0, n_rows, returned, 0)

    def merge(p):
        pm_copy(p, p).wait_recv()
        out_b[...] = jnp.maximum(out_b[...], pm_r[p])

    peers(n_cols, c, merge)

    def sent(b):
        for k in range(chunks):
            hop(b, k, core_sem, partner).wait_send()

    for k in range(chunks):
        hop(r, k, core_sem, partner).wait_send()

        @pl.when(z < half)
        def _():
            hop(r, k, up_sem, r + 2).wait_send()

        @pl.when(z > half)
        def _():
            hop(r, k, down_sem, r - 2).wait_send()

        peers(n_cols, c, lambda p: x_copy(k, p, c).wait_send())

    def drained(s, carry):
        @pl.when(below_ok(s))
        def _():
            b = r - 2 * s
            sent(b)
            cm_copy(b, r).wait_send()
            cm_copy((b // 2) * 2 + 1 - core, r).wait_send()

            @pl.when(z < depth - 1)
            def _():
                for k in range(chunks):
                    hop(b, k, up_sem, r + 2).wait_send()

        @pl.when(above_ok(s))
        def _():
            b = r + 2 * s
            sent(b)
            cm_copy(b, r).wait_send()
            cm_copy((b // 2) * 2 + 1 - core, r).wait_send()

            @pl.when(z > half)
            def _():
                for k in range(chunks):
                    hop(b, k, down_sem, r - 2).wait_send()
        return carry

    lax.fori_loop(1, depth, drained, 0)

    def row_sent(p):
        me_copy(p, r).wait_send()
        sm_copy(p, r).wait_send()
        rs_copy(p, r).wait_send()

    peers(n_rows, r, row_sent)

    def col_sent(p):
        xo_copy(p, c).wait_send()
        pm_copy(p, c).wait_send()

    peers(n_cols, c, col_sent)


def local(n_rows, n_cols, big_emb, big_order, small_emb, small_clus, small_order):
    block, dim = big_emb.shape
    cap = small_emb.shape[2]
    width = n_rows * cap
    chunks = block // LANES
    depth = n_rows // 2
    meta = max(block, width)
    bf16, f32, i32 = jnp.bfloat16, jnp.float32, jnp.int32
    dma = pltpu.SemaphoreType.DMA
    vmem = pl.BlockSpec(memory_space=pltpu.VMEM)
    big, small = pl.pallas_call(
        functools.partial(kernel, n_rows, n_cols),
        out_shape=(
            jax.ShapeDtypeStruct((1, block), f32),
            jax.ShapeDtypeStruct((1, n_rows, cap), f32),
        ),
        in_specs=[vmem] * 5,
        out_specs=(vmem, vmem),
        scratch_shapes=[
            pltpu.VMEM((n_rows, block, dim), bf16),
            pltpu.VMEM((n_cols, block, dim), bf16),
            pltpu.VMEM((n_cols, 1, block), i32),
            pltpu.VMEM((n_rows, 8, meta), i32),
            pltpu.VMEM((n_rows, 8, meta), i32),
            pltpu.VMEM((n_rows, cap, dim), bf16),
            pltpu.VMEM((n_rows, cap, dim), bf16),
            pltpu.VMEM((8, n_cols * block), f32),
            pltpu.VMEM((n_cols, 1, block), f32),
            pltpu.VMEM((n_cols, 1, block), f32),
            pltpu.VMEM((n_rows, 1, block), f32),
            pltpu.VMEM((n_rows, 1, block), f32),
            pltpu.VMEM((1, width), f32),
            pltpu.VMEM((n_rows, 1, width), f32),
            pltpu.VMEM((2, n_rows, width), i32),
            dma((n_rows, chunks)),
            dma((depth, chunks)),
            dma((depth, chunks)),
            dma((depth, chunks)),
            dma((n_cols, chunks)),
            dma((n_cols, chunks)),
            dma((n_cols,)),
            dma((n_cols,)),
            dma((n_rows,)),
            dma((n_rows,)),
            dma((n_rows,)),
            dma((n_rows,)),
            dma((n_rows,)),
            dma((n_rows,)),
            dma((n_cols,)),
            dma((n_cols,)),
            dma((n_rows,)),
            dma((n_rows,)),
        ],
        compiler_params=pltpu.CompilerParams(
            collective_id=0, has_side_effects=True, vmem_limit_bytes=48 * 1024 * 1024
        ),
    )(big_emb, big_order.reshape(1, block), small_emb, small_clus, small_order)
    return big.reshape(block), small


def solution(mesh):
    placed = (
        P(("groups", "rows", "cols"), None),
        P(("groups", "rows", "cols")),
        P(("groups", "rows", "cols"), None, None, None),
        P(("groups", "rows", "cols"), None, None),
        P(("groups", "rows", "cols"), None, None),
    )
    return jax.shard_map(
        functools.partial(local, mesh.shape["rows"], mesh.shape["cols"]),
        mesh=mesh,
        in_specs=placed,
        out_specs=(P(("groups", "rows", "cols")), P(("groups", "rows", "cols"), None, None)),
        check_vma=False,
    )
```

```python
import functools

import jax
import jax.numpy as jnp
from jax import lax
from jax.experimental import pallas as pl
from jax.experimental.pallas import tpu as pltpu
from jax.sharding import PartitionSpec as P

LANES = 128
PIECE = 64
MESH = pl.DeviceIdType.MESH


def normalize(values):
    floats = values.astype(jnp.float32)
    squares = jnp.sum(floats * floats, axis=-1, keepdims=True)
    return (floats * lax.rsqrt(squares + 1e-06)).astype(jnp.bfloat16)


def upright(row):
    return jnp.broadcast_to(row, (LANES, LANES)).T


def kernel(
    n_rows, n_cols,
    be_in, bo_in, se_in, sc_in, so_in, out_b, out_s,
    be, bo, se, sc, so, in_sem, col_buf, row_buf, row_ord, meta_s, meta_r, sm_s, sm_r, acc, pm_s, pm_r, cm_s, cm_r, rs_s, rs_r, pad,
    recv, up_sem, down_sem, core_sem, x_send, x_recv, xo_send, xo_recv,
    me_send, me_recv, sm_send, sm_recv, rs_send, rs_recv, pm_send, pm_recv, cm_send, cm_recv,
):
    fetches = [
        pltpu.make_async_copy(src, dst, in_sem.at[at])
        for at, (src, dst) in enumerate(((be_in, be), (bo_in, bo), (sc_in, sc), (so_in, so), (se_in, se)))
    ]
    for fetch in fetches:
        fetch.start()
    r = lax.axis_index("rows")
    c = lax.axis_index("cols")
    z, core = r // 2, r % 2
    partner = z * 2 + 1 - core
    depth, half = n_rows // 2, n_rows // 4
    block = be.shape[0]
    chunks = block // PIECE
    ratio = LANES // PIECE
    cap = se.shape[2]
    width = rs_s.shape[1]

    def peers(count, me, body):
        def one(d, carry):
            body(lax.rem(me + d, count))
            return carry
        lax.fori_loop(1, count, one, 0)

    barrier = pltpu.get_barrier_semaphore()
    peers(n_rows, r, lambda p: pl.semaphore_signal(barrier, inc=1, device_id={"rows": p}, device_id_type=MESH))
    peers(n_cols, c, lambda p: pl.semaphore_signal(barrier, inc=1, device_id={"cols": p}, device_id_type=MESH))

    def remote(src, dst, send, recv_sem, axis, to):
        return pltpu.make_async_remote_copy(
            src_ref=src, dst_ref=dst, send_sem=send, recv_sem=recv_sem, device_id={axis: to}, device_id_type=MESH
        )

    def part(b, k):
        return col_buf.at[b, pl.ds(k * PIECE, PIECE), :]

    def hop(b, k, sems, to):
        return remote(part(b, k), part(b, k), sems.at[b // 2, k], recv.at[b, k], "rows", to)

    def x_copy(k, to, owner):
        lines = pl.ds(k * PIECE, PIECE)
        return remote(part(r, k), row_buf.at[owner, lines, :], x_send.at[to, k], x_recv.at[owner, k], "cols", to)

    def xo_copy(to, owner):
        return remote(bo, row_ord.at[owner], xo_send.at[to], xo_recv.at[owner], "cols", to)

    def me_copy(to, owner):
        return remote(meta_s.at[to], meta_r.at[owner], me_send.at[to], me_recv.at[owner], "rows", to)

    def sm_copy(to, owner):
        return remote(sm_s.at[to], sm_r.at[owner], sm_send.at[to], sm_recv.at[owner], "rows", to)

    def rs_copy(to, owner):
        return remote(rs_s, rs_r.at[owner], rs_send.at[to], rs_recv.at[owner], "rows", to)

    def pm_copy(to, owner):
        return remote(pm_s.at[to], pm_r.at[owner], pm_send.at[to], pm_recv.at[owner], "cols", to)

    def cm_copy(to, owner):
        return remote(cm_s.at[to], cm_r.at[owner], cm_send.at[to], cm_recv.at[owner], "rows", to)

    def below_ok(s):
        return (z - s >= 0) & (z - s < half)

    def above_ok(s):
        return (z + s < depth) & (z >= half)

    fetches[0].wait()

    for k in range(chunks):
        lines = pl.ds(k * PIECE, PIECE)
        unit = normalize(be[lines, :])
        col_buf[r, lines, :] = unit
        row_buf[c, lines, :] = unit
        if k == 0:
            pl.semaphore_wait(barrier, n_rows - 1 + n_cols - 1)

        @pl.when(z < half)
        def _():
            hop(r, k, up_sem, r + 2).start()

        @pl.when(z > half)
        def _():
            hop(r, k, down_sem, r - 2).start()

        hop(r, k, core_sem, partner).start()
        peers(n_cols, c, lambda p: x_copy(k, p, c).start())

    for fetch in fetches[1:4]:
        fetch.wait()
    row_ord[c] = bo[...]
    peers(n_cols, c, lambda p: xo_copy(p, c).start())

    pad[...] = jnp.zeros_like(pad)
    pad[0, :, :cap] = sc[0]
    pad[1, :, :cap] = so[0]
    clus = pltpu.roll(pad[0], r * cap, 1)
    order = pltpu.roll(pad[1], r * cap, 1)
    for p in range(n_rows):
        meta_s[p, 0:1, :block] = bo[...]
        meta_s[p, 1:2, :width] = clus[p:p + 1, :]
        meta_s[p, 2:3, :width] = order[p:p + 1, :]
    peers(n_rows, r, lambda p: me_copy(p, r).start())
    fetches[4].wait()
    sm_s[...] = normalize(se[0])

    @pl.when(z >= half)
    def _():
        peers(n_rows, r, lambda p: sm_copy(p, r).start())

    meta_r[r] = meta_s[r]
    sm_r[r] = sm_s[r]
    acc[...] = jnp.full(acc.shape, -1.0, jnp.float32)

    def forward(s, k):
        @pl.when(below_ok(s))
        def _():
            b = r - 2 * s
            hop(b, k, core_sem, partner).wait_recv()

            @pl.when(z < depth - 1)
            def _():
                hop(b, k, up_sem, r + 2).start()

            hop(b, k, core_sem, partner).start()

        @pl.when(above_ok(s))
        def _():
            b = r + 2 * s
            hop(b, k, core_sem, partner).wait_recv()

            @pl.when(z > half)
            def _():
                hop(b, k, down_sem, r - 2).start()

            hop(b, k, core_sem, partner).start()

    def scores_of(b, k, both):
        at = pl.ds(k * LANES, LANES)
        ord_col = upright(meta_r[b, 0:1, at])
        rows = row_buf[...].reshape(n_cols * block, row_buf.shape[2])
        scores = lax.dot_general(
            col_buf[b, at, :], rows, (((1,), (1,)), ((), ())), preferred_element_type=jnp.float32
        )
        best = jnp.full((LANES, LANES), -1.0, jnp.float32)
        for tile in range(n_cols * block // LANES):
            lanes = slice(tile * LANES, (tile + 1) * LANES)
            here = scores[:, lanes]
            lane = (tile * LANES) % block
            ord_row = row_ord[tile * LANES // block, 0:1, lane:lane + LANES]
            kept = jnp.where(ord_col < ord_row, here, jnp.float32(-1.0))
            acc[:, lanes] = jnp.maximum(acc[:, lanes], jnp.max(kept.reshape(LANES // 8, 8, LANES), axis=0))
            if both:
                best = jnp.maximum(best, jnp.where(ord_row < ord_col, here, jnp.float32(-1.0)))
        if both:
            cm_s[b, 0:1, at] = jnp.max(best.T, axis=0, keepdims=True)

    def pair(b, k):
        other = (b // 2) * 2 + 1 - core
        for piece in range(k * ratio, (k + 1) * ratio):
            hop(other, piece, core_sem, partner).wait_recv()
        scores_of(b, k, True)
        scores_of(other, k, True)
        if k == chunks // ratio - 1:
            cm_copy(b, r).start()
            cm_copy(other, r).start()

    def pairs(s, k):
        @pl.when(below_ok(s))
        def _():
            pair(r - 2 * s, k)

        @pl.when(above_ok(s))
        def _():
            pair(r + 2 * s, k)

    if depth > 1:
        for k in range(chunks):
            forward(1, k)
    for k in range(chunks):
        peers(n_cols, c, lambda p: x_copy(k, p, p).wait_recv())
    peers(n_cols, c, lambda p: xo_copy(p, p).wait_recv())
    peers(n_rows, r, lambda p: me_copy(p, p).wait_recv())
    for k in range(chunks):
        hop(partner, k, core_sem, partner).wait_recv()
    for k in range(chunks // ratio):
        scores_of(r, k, False)
        scores_of(partner, k, False)

    @pl.when(z < half)
    def _():
        peers(n_rows, r, lambda p: sm_copy(p, r).start())

    def step(s, carry):
        for k in range(chunks):
            forward(s, k)
            if k % ratio == ratio - 1:
                pairs(s - 1, k // ratio)
        return carry

    lax.fori_loop(2, depth, step, 0)
    peers(n_rows, r, lambda p: sm_copy(p, p).wait_recv())
    slots = n_rows * cap
    clus_row = jnp.sum(meta_r[:, 1, :width], axis=0, keepdims=True)
    ord_row = jnp.sum(meta_r[:, 2, :width], axis=0, keepdims=True)
    emb = sm_r[...].reshape(slots, sm_r.shape[2])
    best = jnp.full((1, width), -1.0, jnp.float32)
    for at in range(0, slots, LANES):
        scores = lax.dot_general(
            emb[at:at + LANES], emb, (((1,), (1,)), ((), ())), preferred_element_type=jnp.float32
        )
        clus_col = jnp.broadcast_to(upright(clus_row[:, at:at + LANES])[:, :1], (LANES, width))
        ord_col = jnp.broadcast_to(upright(ord_row[:, at:at + LANES])[:, :1], (LANES, width))
        allowed = (clus_col == clus_row) & (clus_row >= 0) & (ord_col < ord_row)
        kept = jnp.where(allowed, scores, jnp.float32(-1.0))
        best = jnp.maximum(best, jnp.max(kept, axis=0, keepdims=True))
    rs_s[...] = best
    rs_r[r] = best
    peers(n_rows, r, lambda p: rs_copy(p, r).start())

    for k in range(chunks // ratio):
        pairs(depth - 1, k)

    final = jnp.max(acc[...], axis=0, keepdims=True)
    for p in range(n_cols):
        pm_s[p] = final[:, p * block:(p + 1) * block]
    peers(n_cols, c, lambda p: pm_copy(p, c).start())

    peers(n_rows, r, lambda p: rs_copy(p, p).wait_recv())
    back = pltpu.roll(rs_r[:, 0, :], lax.rem(width - r * cap, width), 1)
    out_s[0] = back[:, :cap]

    def sent(b):
        for k in range(chunks):
            hop(b, k, core_sem, partner).wait_send()

    for k in range(chunks):
        hop(r, k, core_sem, partner).wait_send()

        @pl.when(z < half)
        def _():
            hop(r, k, up_sem, r + 2).wait_send()

        @pl.when(z > half)
        def _():
            hop(r, k, down_sem, r - 2).wait_send()

        peers(n_cols, c, lambda p: x_copy(k, p, c).wait_send())

    def drained(s, carry):
        @pl.when(below_ok(s))
        def _():
            b = r - 2 * s
            sent(b)
            cm_copy(b, r).wait_send()
            cm_copy((b // 2) * 2 + 1 - core, r).wait_send()

            @pl.when(z < depth - 1)
            def _():
                for k in range(chunks):
                    hop(b, k, up_sem, r + 2).wait_send()

        @pl.when(above_ok(s))
        def _():
            b = r + 2 * s
            sent(b)
            cm_copy(b, r).wait_send()
            cm_copy((b // 2) * 2 + 1 - core, r).wait_send()

            @pl.when(z > half)
            def _():
                for k in range(chunks):
                    hop(b, k, down_sem, r - 2).wait_send()
        return carry

    lax.fori_loop(1, depth, drained, 0)

    def row_sent(p):
        me_copy(p, r).wait_send()
        sm_copy(p, r).wait_send()
        rs_copy(p, r).wait_send()

    peers(n_rows, r, row_sent)

    out_b[...] = pm_s[c]

    def returned(p, carry):
        zp = p // 2
        low = (z < half) & (zp > z)
        high = (z >= half) & (zp >= half) & (zp < z)

        @pl.when(low | high)
        def _():
            cm_copy(p, p).wait_recv()
            out_b[...] = jnp.maximum(out_b[...], cm_r[p])
        return carry

    lax.fori_loop(0, n_rows, returned, 0)

    def merge(p):
        pm_copy(p, p).wait_recv()
        out_b[...] = jnp.maximum(out_b[...], pm_r[p])

    peers(n_cols, c, merge)

    def col_sent(p):
        xo_copy(p, c).wait_send()
        pm_copy(p, c).wait_send()

    peers(n_cols, c, col_sent)


def local(n_rows, n_cols, big_emb, big_order, small_emb, small_clus, small_order):
    block, dim = big_emb.shape
    cap = small_emb.shape[2]
    width = n_rows * cap
    chunks = block // PIECE
    depth = n_rows // 2
    meta = max(block, width)
    bf16, f32, i32 = jnp.bfloat16, jnp.float32, jnp.int32
    dma = pltpu.SemaphoreType.DMA
    vmem = pl.BlockSpec(memory_space=pltpu.VMEM)
    big, small = pl.pallas_call(
        functools.partial(kernel, n_rows, n_cols),
        out_shape=(
            jax.ShapeDtypeStruct((1, block), f32),
            jax.ShapeDtypeStruct((1, n_rows, cap), f32),
        ),
        in_specs=[pl.BlockSpec(memory_space=pl.ANY)] * 5,
        out_specs=(vmem, vmem),
        scratch_shapes=[
            pltpu.VMEM(big_emb.shape, bf16),
            pltpu.VMEM((1, block), i32),
            pltpu.VMEM(small_emb.shape, bf16),
            pltpu.VMEM(small_clus.shape, i32),
            pltpu.VMEM(small_order.shape, i32),
            dma((5,)),
            pltpu.VMEM((n_rows, block, dim), bf16),
            pltpu.VMEM((n_cols, block, dim), bf16),
            pltpu.VMEM((n_cols, 1, block), i32),
            pltpu.VMEM((n_rows, 8, meta), i32),
            pltpu.VMEM((n_rows, 8, meta), i32),
            pltpu.VMEM((n_rows, cap, dim), bf16),
            pltpu.VMEM((n_rows, cap, dim), bf16),
            pltpu.VMEM((8, n_cols * block), f32),
            pltpu.VMEM((n_cols, 1, block), f32),
            pltpu.VMEM((n_cols, 1, block), f32),
            pltpu.VMEM((n_rows, 1, block), f32),
            pltpu.VMEM((n_rows, 1, block), f32),
            pltpu.VMEM((1, width), f32),
            pltpu.VMEM((n_rows, 1, width), f32),
            pltpu.VMEM((2, n_rows, width), i32),
            dma((n_rows, chunks)),
            dma((depth, chunks)),
            dma((depth, chunks)),
            dma((depth, chunks)),
            dma((n_cols, chunks)),
            dma((n_cols, chunks)),
            dma((n_cols,)),
            dma((n_cols,)),
            dma((n_rows,)),
            dma((n_rows,)),
            dma((n_rows,)),
            dma((n_rows,)),
            dma((n_rows,)),
            dma((n_rows,)),
            dma((n_cols,)),
            dma((n_cols,)),
            dma((n_rows,)),
            dma((n_rows,)),
        ],
        compiler_params=pltpu.CompilerParams(
            collective_id=0, has_side_effects=True, vmem_limit_bytes=60 * 1024 * 1024
        ),
    )(big_emb, big_order.reshape(1, block), small_emb, small_clus, small_order)
    return big.reshape(block), small


def solution(mesh):
    placed = (
        P(("groups", "rows", "cols"), None),
        P(("groups", "rows", "cols")),
        P(("groups", "rows", "cols"), None, None, None),
        P(("groups", "rows", "cols"), None, None),
        P(("groups", "rows", "cols"), None, None),
    )
    return jax.shard_map(
        functools.partial(local, mesh.shape["rows"], mesh.shape["cols"]),
        mesh=mesh,
        in_specs=placed,
        out_specs=(P(("groups", "rows", "cols")), P(("groups", "rows", "cols"), None, None)),
        check_vma=False,
    )
```

```python
import functools

import jax
import jax.numpy as jnp
from jax import lax
from jax.experimental import pallas as pl
from jax.experimental.pallas import tpu as pltpu
from jax.sharding import PartitionSpec as P

LANES = 128
PIECE = 32
MESH = pl.DeviceIdType.MESH


def normalize(values):
    floats = values.astype(jnp.float32)
    squares = jnp.sum(floats * floats, axis=-1, keepdims=True)
    return (floats * lax.rsqrt(squares + 1e-06)).astype(jnp.bfloat16)


def upright(row):
    return jnp.broadcast_to(row, (LANES, LANES)).T


def kernel(
    n_rows, n_cols,
    be_in, bo_in, se_in, sc_in, so_in, out_b_hbm, out_s_hbm,
    out_b, out_s, out_sem, be, bo, se, sc, so, in_sem, col_buf, row_buf, row_ord, meta_s, meta_r, sm_s, sm_r, acc, pm_s, pm_r, cm_s, cm_r, rs_s, rs_r, pad,
    recv, up_sem, down_sem, core_sem, x_send, x_recv, xo_send, xo_recv,
    me_send, me_recv, sm_send, sm_recv, rs_send, rs_recv, pm_send, pm_recv, cm_send, cm_recv,
):
    fetches = [
        pltpu.make_async_copy(src, dst, in_sem.at[at])
        for at, (src, dst) in enumerate(((be_in, be), (bo_in, bo), (sc_in, sc), (so_in, so), (se_in, se)))
    ]
    for fetch in fetches:
        fetch.start()
    r = lax.axis_index("rows")
    c = lax.axis_index("cols")
    z, core = r // 2, r % 2
    partner = z * 2 + 1 - core
    depth, half = n_rows // 2, max(n_rows // 4 - 1, 0)
    block = be.shape[0]
    chunks = block // PIECE
    ratio = LANES // PIECE
    cap = se.shape[2]
    width = rs_s.shape[1]

    def peers(count, me, body):
        def one(d, carry):
            body(lax.rem(me + d, count))
            return carry
        lax.fori_loop(1, count, one, 0)

    barrier = pltpu.get_barrier_semaphore()
    peers(n_rows, r, lambda p: pl.semaphore_signal(barrier, inc=1, device_id={"rows": p}, device_id_type=MESH))
    peers(n_cols, c, lambda p: pl.semaphore_signal(barrier, inc=1, device_id={"cols": p}, device_id_type=MESH))

    def remote(src, dst, send, recv_sem, axis, to):
        return pltpu.make_async_remote_copy(
            src_ref=src, dst_ref=dst, send_sem=send, recv_sem=recv_sem, device_id={axis: to}, device_id_type=MESH
        )

    def part(b, k):
        return col_buf.at[b, pl.ds(k * PIECE, PIECE), :]

    def hop(b, k, sems, to):
        return remote(part(b, k), part(b, k), sems.at[b // 2, k], recv.at[b, k], "rows", to)

    def x_copy(k, to, owner):
        lines = pl.ds(k * PIECE, PIECE)
        return remote(part(r, k), row_buf.at[owner, lines, :], x_send.at[to, k], x_recv.at[owner, k], "cols", to)

    def xo_copy(to, owner):
        return remote(bo, row_ord.at[owner], xo_send.at[to], xo_recv.at[owner], "cols", to)

    def me_copy(to, owner):
        return remote(meta_s.at[to], meta_r.at[owner], me_send.at[to], me_recv.at[owner], "rows", to)

    def sm_copy(to, owner):
        return remote(sm_s.at[to], sm_r.at[owner], sm_send.at[to], sm_recv.at[owner], "rows", to)

    def rs_copy(to, owner):
        return remote(rs_s, rs_r.at[owner], rs_send.at[to], rs_recv.at[owner], "rows", to)

    def pm_copy(to, owner):
        return remote(pm_s.at[to], pm_r.at[owner], pm_send.at[to], pm_recv.at[owner], "cols", to)

    def cm_copy(to, owner):
        return remote(cm_s.at[to], cm_r.at[owner], cm_send.at[to], cm_recv.at[owner], "rows", to)

    def below_ok(s):
        return (z - s >= 0) & (z - s < half)

    def above_ok(s):
        return (z + s < depth) & (z >= half)

    fetches[0].wait()

    for k in range(chunks):
        lines = pl.ds(k * PIECE, PIECE)
        unit = normalize(be[lines, :])
        col_buf[r, lines, :] = unit
        row_buf[c, lines, :] = unit
        if k == 0:
            pl.semaphore_wait(barrier, n_rows - 1 + n_cols - 1)

        @pl.when(z < half)
        def _():
            hop(r, k, up_sem, r + 2).start()

        @pl.when(z > half)
        def _():
            hop(r, k, down_sem, r - 2).start()

        hop(r, k, core_sem, partner).start()
        peers(n_cols, c, lambda p: x_copy(k, p, c).start())

    for fetch in fetches[1:4]:
        fetch.wait()
    row_ord[c] = bo[...]
    peers(n_cols, c, lambda p: xo_copy(p, c).start())

    pad[...] = jnp.zeros_like(pad)
    pad[0, :, :cap] = sc[0]
    pad[1, :, :cap] = so[0]
    clus = pltpu.roll(pad[0], r * cap, 1)
    order = pltpu.roll(pad[1], r * cap, 1)
    for p in range(n_rows):
        meta_s[p, 0:1, :block] = bo[...]
        meta_s[p, 1:2, :width] = clus[p:p + 1, :]
        meta_s[p, 2:3, :width] = order[p:p + 1, :]
    peers(n_rows, r, lambda p: me_copy(p, r).start())
    fetches[4].wait()
    sm_s[...] = normalize(se[0])

    @pl.when(z <= half)
    def _():
        peers(n_rows, r, lambda p: sm_copy(p, r).start())

    meta_r[r] = meta_s[r]
    sm_r[r] = sm_s[r]
    acc[...] = jnp.full(acc.shape, -1.0, jnp.float32)

    def forward(s, k):
        @pl.when(below_ok(s))
        def _():
            b = r - 2 * s
            hop(b, k, core_sem, partner).wait_recv()

            @pl.when(z < depth - 1)
            def _():
                hop(b, k, up_sem, r + 2).start()

            hop(b, k, core_sem, partner).start()

        @pl.when(above_ok(s))
        def _():
            b = r + 2 * s
            hop(b, k, core_sem, partner).wait_recv()

            @pl.when(z > half)
            def _():
                hop(b, k, down_sem, r - 2).start()

            hop(b, k, core_sem, partner).start()

    def scores_of(b, k, both):
        at = pl.ds(k * LANES, LANES)
        ord_col = upright(meta_r[b, 0:1, at])
        rows = row_buf[...].reshape(n_cols * block, row_buf.shape[2])
        scores = lax.dot_general(
            col_buf[b, at, :], rows, (((1,), (1,)), ((), ())), preferred_element_type=jnp.float32
        )
        best = jnp.full((LANES, LANES), -1.0, jnp.float32)
        for tile in range(n_cols * block // LANES):
            lanes = slice(tile * LANES, (tile + 1) * LANES)
            here = scores[:, lanes]
            lane = (tile * LANES) % block
            ord_row = row_ord[tile * LANES // block, 0:1, lane:lane + LANES]
            kept = jnp.where(ord_col < ord_row, here, jnp.float32(-1.0))
            acc[:, lanes] = jnp.maximum(acc[:, lanes], jnp.max(kept.reshape(LANES // 8, 8, LANES), axis=0))
            if both:
                best = jnp.maximum(best, jnp.where(ord_row < ord_col, here, jnp.float32(-1.0)))
        if both:
            cm_s[b, 0:1, at] = jnp.max(best.T, axis=0, keepdims=True)

    def pair(b, k):
        other = (b // 2) * 2 + 1 - core
        for piece in range(k * ratio, (k + 1) * ratio):
            hop(other, piece, core_sem, partner).wait_recv()
        scores_of(b, k, True)
        scores_of(other, k, True)
        if k == chunks // ratio - 1:
            cm_copy(b, r).start()
            cm_copy(other, r).start()

    def pairs(s, k):
        @pl.when(below_ok(s))
        def _():
            pair(r - 2 * s, k)

        @pl.when(above_ok(s))
        def _():
            pair(r + 2 * s, k)

    if depth > 1:
        for k in range(chunks):
            forward(1, k)
    for k in range(chunks):
        peers(n_cols, c, lambda p: x_copy(k, p, p).wait_recv())
    peers(n_cols, c, lambda p: xo_copy(p, p).wait_recv())
    peers(n_rows, r, lambda p: me_copy(p, p).wait_recv())
    for k in range(chunks):
        hop(partner, k, core_sem, partner).wait_recv()
    for k in range(chunks // ratio):
        scores_of(r, k, False)
        scores_of(partner, k, False)

    @pl.when(z > half)
    def _():
        peers(n_rows, r, lambda p: sm_copy(p, r).start())

    def step(s, carry):
        for k in range(chunks):
            forward(s, k)
            if k % ratio == ratio - 1:
                pairs(s - 1, k // ratio)
        return carry

    lax.fori_loop(2, depth, step, 0)
    peers(n_rows, r, lambda p: sm_copy(p, p).wait_recv())
    slots = n_rows * cap
    clus_row = jnp.sum(meta_r[:, 1, :width], axis=0, keepdims=True)
    ord_row = jnp.sum(meta_r[:, 2, :width], axis=0, keepdims=True)
    emb = sm_r[...].reshape(slots, sm_r.shape[2])
    best = jnp.full((1, width), -1.0, jnp.float32)
    for at in range(0, slots, LANES):
        scores = lax.dot_general(
            emb[at:at + LANES], emb, (((1,), (1,)), ((), ())), preferred_element_type=jnp.float32
        )
        clus_col = jnp.broadcast_to(upright(clus_row[:, at:at + LANES])[:, :1], (LANES, width))
        ord_col = jnp.broadcast_to(upright(ord_row[:, at:at + LANES])[:, :1], (LANES, width))
        allowed = (clus_col == clus_row) & (clus_row >= 0) & (ord_col < ord_row)
        kept = jnp.where(allowed, scores, jnp.float32(-1.0))
        best = jnp.maximum(best, jnp.max(kept, axis=0, keepdims=True))
    rs_s[...] = best
    rs_r[r] = best
    peers(n_rows, r, lambda p: rs_copy(p, r).start())

    for k in range(chunks // ratio):
        pairs(depth - 1, k)

    final = jnp.max(acc[...], axis=0, keepdims=True)
    for p in range(n_cols):
        pm_s[p] = final[:, p * block:(p + 1) * block]
    peers(n_cols, c, lambda p: pm_copy(p, c).start())

    peers(n_rows, r, lambda p: rs_copy(p, p).wait_recv())
    back = pltpu.roll(rs_r[:, 0, :], lax.rem(width - r * cap, width), 1)
    out_s[0] = back[:, :cap]
    small_out = pltpu.make_async_copy(out_s, out_s_hbm, out_sem.at[1])
    small_out.start()

    def sent(b):
        for k in range(chunks):
            hop(b, k, core_sem, partner).wait_send()

    for k in range(chunks):
        hop(r, k, core_sem, partner).wait_send()

        @pl.when(z < half)
        def _():
            hop(r, k, up_sem, r + 2).wait_send()

        @pl.when(z > half)
        def _():
            hop(r, k, down_sem, r - 2).wait_send()

        peers(n_cols, c, lambda p: x_copy(k, p, c).wait_send())

    def drained(s, carry):
        @pl.when(below_ok(s))
        def _():
            b = r - 2 * s
            sent(b)
            cm_copy(b, r).wait_send()
            cm_copy((b // 2) * 2 + 1 - core, r).wait_send()

            @pl.when(z < depth - 1)
            def _():
                for k in range(chunks):
                    hop(b, k, up_sem, r + 2).wait_send()

        @pl.when(above_ok(s))
        def _():
            b = r + 2 * s
            sent(b)
            cm_copy(b, r).wait_send()
            cm_copy((b // 2) * 2 + 1 - core, r).wait_send()

            @pl.when(z > half)
            def _():
                for k in range(chunks):
                    hop(b, k, down_sem, r - 2).wait_send()
        return carry

    lax.fori_loop(1, depth, drained, 0)

    def row_sent(p):
        me_copy(p, r).wait_send()
        sm_copy(p, r).wait_send()
        rs_copy(p, r).wait_send()

    peers(n_rows, r, row_sent)

    out_b[...] = pm_s[c]

    def returned(p, carry):
        zp = p // 2
        low = (z < half) & (zp > z)
        high = (z >= half) & (zp >= half) & (zp < z)

        @pl.when(low | high)
        def _():
            cm_copy(p, p).wait_recv()
            out_b[...] = jnp.maximum(out_b[...], cm_r[p])
        return carry

    lax.fori_loop(0, n_rows, returned, 0)

    def merge(p):
        pm_copy(p, p).wait_recv()
        out_b[...] = jnp.maximum(out_b[...], pm_r[p])

    peers(n_cols, c, merge)

    def col_sent(p):
        xo_copy(p, c).wait_send()
        pm_copy(p, c).wait_send()

    big_out = pltpu.make_async_copy(out_b, out_b_hbm, out_sem.at[0])
    big_out.start()
    peers(n_cols, c, col_sent)
    small_out.wait()
    big_out.wait()


def local(n_rows, n_cols, big_emb, big_order, small_emb, small_clus, small_order):
    block, dim = big_emb.shape
    cap = small_emb.shape[2]
    width = n_rows * cap
    chunks = block // PIECE
    depth = n_rows // 2
    meta = max(block, width)
    bf16, f32, i32 = jnp.bfloat16, jnp.float32, jnp.int32
    dma = pltpu.SemaphoreType.DMA
    hbm = pl.BlockSpec(memory_space=pltpu.HBM)
    big, small = pl.pallas_call(
        functools.partial(kernel, n_rows, n_cols),
        out_shape=(
            jax.ShapeDtypeStruct((1, block), f32),
            jax.ShapeDtypeStruct((1, n_rows, cap), f32),
        ),
        in_specs=[hbm] * 5,
        out_specs=(hbm, hbm),
        scratch_shapes=[
            pltpu.VMEM((1, block), f32),
            pltpu.VMEM((1, n_rows, cap), f32),
            dma((2,)),
            pltpu.VMEM(big_emb.shape, bf16),
            pltpu.VMEM((1, block), i32),
            pltpu.VMEM(small_emb.shape, bf16),
            pltpu.VMEM(small_clus.shape, i32),
            pltpu.VMEM(small_order.shape, i32),
            dma((5,)),
            pltpu.VMEM((n_rows, block, dim), bf16),
            pltpu.VMEM((n_cols, block, dim), bf16),
            pltpu.VMEM((n_cols, 1, block), i32),
            pltpu.VMEM((n_rows, 8, meta), i32),
            pltpu.VMEM((n_rows, 8, meta), i32),
            pltpu.VMEM((n_rows, cap, dim), bf16),
            pltpu.VMEM((n_rows, cap, dim), bf16),
            pltpu.VMEM((8, n_cols * block), f32),
            pltpu.VMEM((n_cols, 1, block), f32),
            pltpu.VMEM((n_cols, 1, block), f32),
            pltpu.VMEM((n_rows, 1, block), f32),
            pltpu.VMEM((n_rows, 1, block), f32),
            pltpu.VMEM((1, width), f32),
            pltpu.VMEM((n_rows, 1, width), f32),
            pltpu.VMEM((2, n_rows, width), i32),
            dma((n_rows, chunks)),
            dma((depth, chunks)),
            dma((depth, chunks)),
            dma((depth, chunks)),
            dma((n_cols, chunks)),
            dma((n_cols, chunks)),
            dma((n_cols,)),
            dma((n_cols,)),
            dma((n_rows,)),
            dma((n_rows,)),
            dma((n_rows,)),
            dma((n_rows,)),
            dma((n_rows,)),
            dma((n_rows,)),
            dma((n_cols,)),
            dma((n_cols,)),
            dma((n_rows,)),
            dma((n_rows,)),
        ],
        compiler_params=pltpu.CompilerParams(
            collective_id=0, has_side_effects=True, vmem_limit_bytes=60 * 1024 * 1024
        ),
    )(big_emb, big_order.reshape(1, block), small_emb, small_clus, small_order)
    return big.reshape(block), small


def solution(mesh):
    placed = (
        P(("groups", "rows", "cols"), None),
        P(("groups", "rows", "cols")),
        P(("groups", "rows", "cols"), None, None, None),
        P(("groups", "rows", "cols"), None, None),
        P(("groups", "rows", "cols"), None, None),
    )
    return jax.shard_map(
        functools.partial(local, mesh.shape["rows"], mesh.shape["cols"]),
        mesh=mesh,
        in_specs=placed,
        out_specs=(P(("groups", "rows", "cols")), P(("groups", "rows", "cols"), None, None)),
        check_vma=False,
    )
```
